32 devices in a mesh: rep: 2 (over x), tp: 8 (over z, y), dp: 2 (over core).
Axes of the slice: x: 2, y: 2, z: 4, core: 2. Of those that a mesh axis runs over, the one named last changes fastest.
Arguments:
- tokens: bfloat16 [1024, 4096], P(('rep', 'dp'), 'tp'), parts along dimension 0, may hold values from -6 to 6
- gate_weight: bfloat16 [4096, 14336], P('dp', 'tp'), may hold values from -0.125 to 0.125
- up_weight: bfloat16 [4096, 14336], P('dp', 'tp'), may hold values from -0.125 to 0.125
- down_weight: bfloat16 [14336, 4096], P('tp', 'dp'), may hold values from -0.0625 to 0.0625
- out_grad: bfloat16 [1024, 4096], P(('rep', 'dp'), 'tp'), parts along dimension 0, may hold values from -6 to 6
Outputs:
- output: bfloat16 [1024, 4096], P(('rep', 'dp'), 'tp'), parts along dimension 0
- input_grad: bfloat16 [1024, 4096], P(('rep', 'dp'), 'tp'), parts along dimension 0
- gate_wgrad: bfloat16 [8192, 14336], P(('rep', 'dp'), 'tp'), parts along dimension 0
- up_wgrad: bfloat16 [8192, 14336], P(('rep', 'dp'), 'tp'), parts along dimension 0
- down_wgrad: bfloat16 [14336, 8192], P('tp', ('rep', 'dp')), parts along dimension 1
The draws below stay inside these ranges and needn't reach their ends.
There are 2 independent parts, one for each index of `rep`. The reference program is written for one: setup_inputs(seed, part) draws one part's arguments, and reference() takes and returns one part's arrays. A program takes and returns all parts, laid end to end along the dimension named above; an argument that names none is the same for every part. Nothing has to cross between parts.
All inputs are finite; a program needn't handle non-finite values.
Results may differ from the reference program's by a relative error of at most 0.013.
Values may be sent and summed in bfloat16 or wider, within the bound.
No kernel may reach another device: no remote copies, remote signals or barrier semaphores. Data moves between devices by JAX's collectives and lax.ppermute only.
A program may use at most 256 MiB of HBM per device.

```python
import jax
import jax.numpy as jnp

D = 4096
FF = 14336
TOKENS = 512


def spiked(values, stream_key, source, target, parts, factor):
    owner, partner = [(jnp.arange(values.shape[axis_at]) // (values.shape[axis_at] // parts)).reshape([-1 if axis == axis_at else 1 for axis in range(values.ndim)]) for axis_at in (source, target)]
    chosen = jax.random.permutation(stream_key, parts)[partner]
    strong = (owner == chosen) | (owner == (partner + parts // 2) % parts)
    return jnp.where(strong, factor * values, values)


def steps_of(own_key, extent, pieces, least, largest):
    level, own = 1.0, jax.random.fold_in(own_key, 6)
    for axis_at, parts in pieces:
        draws = jnp.exp(jax.random.uniform(jax.random.fold_in(own, axis_at), (parts,), jnp.float32, least / len(pieces), largest / len(pieces)))
        level = level * jnp.repeat(draws, extent[axis_at] // parts).reshape([-1 if axis == axis_at else 1 for axis in range(len(extent))])
    return level


def noise(rng, extent, spread, limit, cuts=(), dtype=jnp.bfloat16):
    result = jax.random.normal(rng, extent, jnp.float32) * spread
    if len(cuts) > 0:
        result = steps_of(rng, extent, cuts, -0.22, 0.18) * result
    return jnp.clip(result, min=-limit, max=limit).astype(dtype)


def bell_draw_with(stream_key, shape, scale, limit, shards, heavy, dtype=jnp.bfloat16):
    drawn = scale * jax.random.normal(stream_key, shape, jnp.float32)
    if shards:
        drawn = drawn * steps_of(stream_key, shape, shards, -0.22, 0.18)
    return jnp.clip(spiked(drawn, jax.random.fold_in(stream_key, 3), *heavy), -limit, limit).astype(dtype)


def setup_inputs(seed: int = 0, part: int = 0) -> dict:
    splits = jax.random.split(jax.random.key(seed), 6)
    part_splits = jax.random.split(jax.random.fold_in(splits[5], part), 6)
    return {
        "tokens": noise(part_splits[0], (TOKENS, D), 1.0, 6.0, ((0, 2), (1, 8))),
        "gate_weight": bell_draw_with(splits[1], (D, FF), D ** -0.5, 0.125, ((0, 2), (1, 8)), (1, 0, 8, 2.0)),
        "up_weight": bell_draw_with(splits[2], (D, FF), D ** -0.5, 0.125, ((0, 2), (1, 8)), (1, 0, 8, 2.0)),
        "down_weight": bell_draw_with(splits[3], (FF, D), FF ** -0.5, 0.0625, ((0, 8), (1, 2)), (0, 1, 8, 2.0)),
        "out_grad": noise(part_splits[4], (TOKENS, D), 1.0, 6.0, ((0, 2), (1, 8))),
    }


def reference(tokens, gate_weight, up_weight, down_weight, out_grad):
    gate_value = jnp.dot(tokens, gate_weight, preferred_element_type=jnp.float32)
    up_value = jnp.dot(tokens, up_weight, preferred_element_type=jnp.float32)
    sigmoid_gate = jax.nn.sigmoid(gate_value)
    activated = gate_value * sigmoid_gate
    hidden = (activated * up_value).astype(jnp.bfloat16)
    output = jnp.dot(hidden, down_weight, preferred_element_type=jnp.float32).astype(jnp.bfloat16)
    hidden_grad = jnp.dot(out_grad, down_weight.T, preferred_element_type=jnp.float32)
    gate_grad = (hidden_grad * up_value * sigmoid_gate * (1.0 + gate_value * (1.0 - sigmoid_gate))).astype(jnp.bfloat16)
    up_grad = (hidden_grad * activated).astype(jnp.bfloat16)
    input_grad = (jnp.dot(gate_grad, gate_weight.T, preferred_element_type=jnp.float32)
                  + jnp.dot(up_grad, up_weight.T, preferred_element_type=jnp.float32)).astype(jnp.bfloat16)
    gate_wgrad = jnp.dot(tokens.T, gate_grad, preferred_element_type=jnp.float32).astype(jnp.bfloat16)
    up_wgrad = jnp.dot(tokens.T, up_grad, preferred_element_type=jnp.float32).astype(jnp.bfloat16)
    down_wgrad = jnp.dot(hidden.T, out_grad, preferred_element_type=jnp.float32).astype(jnp.bfloat16)
    return output, input_grad, gate_wgrad, up_wgrad, down_wgrad
```

```python
import jax
import jax.numpy as jnp
from jax import lax
from jax.sharding import PartitionSpec as P

BF16 = jnp.bfloat16
F32 = jnp.float32


def ring_at(position, n):
    position = lax.rem(position + 2 * n, n)
    return jnp.where(position < n // 2, 2 * position, 2 * (n - 1 - position) + 1)


def place_of(index, n):
    return jnp.where(lax.rem(index, 2) == 0, index // 2, n - 1 - index // 2)


def hops(n):
    order = list(range(0, n, 2)) + list(range(n - 1, 0, -2))
    up = [(order[i], order[(i + 1) % n]) for i in range(n)]
    return up, [(b, a) for a, b in up]


def swap_cores(value):
    return lax.ppermute(value, "dp", [(0, 1), (1, 0)])


def ring_gather(own, n):
    up, down = hops(n)
    rows = own.shape[0] // 2
    blocks = {0: own}
    a = b = own
    for step in range(1, n // 2):
        a = lax.ppermute(a, "tp", up)
        b = lax.ppermute(b, "tp", down)
        blocks[step], blocks[-step] = a, b
    a = lax.ppermute(a[:rows], "tp", up)
    b = lax.ppermute(b[rows:], "tp", down)
    blocks[n // 2] = jnp.concatenate([a, b], 0)
    return blocks


def place(blocks, n):
    rows, width = blocks[0].shape
    spot = place_of(lax.axis_index("tp"), n)
    whole = jnp.zeros((rows, n * width), blocks[0].dtype)
    for distance, block in blocks.items():
        column = ring_at(spot - distance, n) * width
        whole = lax.dynamic_update_slice(whole, block, (0, column))
    return whole


def to_feature_half(whole):
    half = whole.shape[1] // 2
    core = lax.axis_index("dp")
    keep = lax.dynamic_slice_in_dim(whole, core * half, half, 1)
    send = lax.dynamic_slice_in_dim(whole, (1 - core) * half, half, 1)
    return jnp.concatenate([keep, swap_cores(send)], 0)


def sum_cores(partial):
    rows = partial.shape[0] // 2
    return partial[:rows] + swap_cores(partial[rows:].astype(BF16)).astype(F32)


def with_other_rows(own):
    return jnp.concatenate([own, swap_cores(own)], 0)


def to_token_rows(partial):
    rows, half = partial.shape[0] // 2, partial.shape[1]
    core = lax.axis_index("dp")
    got = swap_cores(partial[rows:])
    whole = jnp.zeros((rows, 2 * half), partial.dtype)
    whole = lax.dynamic_update_slice(whole, partial[:rows], (0, core * half))
    return lax.dynamic_update_slice(whole, got, (0, (1 - core) * half))


def ring_scatter(terms, n):
    up, down = hops(n)
    rows, width = terms.shape[0], terms.shape[1] // n
    cut = rows // 2
    spot = place_of(lax.axis_index("tp"), n)

    def term(distance):
        column = ring_at(spot + distance, n) * width
        return lax.dynamic_slice(terms, (0, column), (rows, width))

    far = term(n // 2)
    a = lax.ppermute(far[:cut], "tp", up)
    b = lax.ppermute(far[cut:], "tp", down)
    for distance in range(n // 2 - 1, 0, -1):
        ahead, behind = term(distance), term(-distance)
        if a.shape[0] == cut:
            a = jnp.concatenate([ahead[:cut] + a, ahead[cut:]], 0)
            b = jnp.concatenate([behind[:cut], behind[cut:] + b], 0)
        else:
            a, b = ahead + a, behind + b
        a = lax.ppermute(a, "tp", up)
        b = lax.ppermute(b, "tp", down)
    return (term(0).astype(F32) + a.astype(F32) + b.astype(F32)).astype(BF16)


def dot(left, right, left_dim, right_dim):
    return lax.dot_general(left, right, (((left_dim,), (right_dim,)), ((), ())), preferred_element_type=F32)


def body(n, tokens, gate_weight, up_weight, down_weight, out_grad):
    tokens_half = to_feature_half(place(ring_gather(tokens, n), n))
    grad_half = to_feature_half(place(ring_gather(out_grad, n), n))

    gate_value = sum_cores(dot(tokens_half, gate_weight, 1, 0))
    up_value = sum_cores(dot(tokens_half, up_weight, 1, 0))
    sigmoid_gate = jax.nn.sigmoid(gate_value)
    activated = gate_value * sigmoid_gate
    hidden = with_other_rows((activated * up_value).astype(BF16))
    output = ring_scatter(to_token_rows(dot(hidden, down_weight, 1, 0).astype(BF16)), n)

    hidden_grad = sum_cores(dot(grad_half, down_weight, 1, 1))
    gate_grad = with_other_rows(
        (hidden_grad * up_value * sigmoid_gate * (1.0 + gate_value * (1.0 - sigmoid_gate))).astype(BF16)
    )
    up_grad = with_other_rows((hidden_grad * activated).astype(BF16))
    in_terms = dot(gate_grad, gate_weight, 1, 1) + dot(up_grad, up_weight, 1, 1)
    input_grad = ring_scatter(to_token_rows(in_terms.astype(BF16)), n)

    gate_wgrad = dot(tokens_half, gate_grad, 0, 0).astype(BF16)
    up_wgrad = dot(tokens_half, up_grad, 0, 0).astype(BF16)
    down_wgrad = dot(hidden, grad_half, 0, 0).astype(BF16)
    return output, input_grad, gate_wgrad, up_wgrad, down_wgrad


def solution(mesh):
    n = mesh.shape["tp"]
    rows = P(("rep", "dp"), "tp")
    in_specs = (rows, P("dp", "tp"), P("dp", "tp"), P("tp", "dp"), rows)
    out_specs = (rows, rows, rows, rows, P("tp", ("rep", "dp")))

    def call(*args):
        return body(n, *args)

    return jax.shard_map(call, mesh=mesh, in_specs=in_specs, out_specs=out_specs, check_vma=False)
```

```python
import jax
import jax.numpy as jnp
from jax import lax
from jax.sharding import PartitionSpec as P

BF16 = jnp.bfloat16
F32 = jnp.float32


def hops(n):
    order = list(range(0, n, 2)) + list(range(n - 1, 0, -2))
    up = [(order[i], order[(i + 1) % n]) for i in range(n)]
    return up, [(b, a) for a, b in up]


class Ring:
    def __init__(self, n):
        self.n, self.m = n, n // 2
        self.up_hops, self.down_hops = hops(n)
        index = lax.axis_index("tp")
        self.core = lax.axis_index("dp")
        self.spot = jnp.where(lax.rem(index, 2) == 0, index // 2, n - 1 - index // 2)

    def up(self, value):
        return lax.ppermute(value, "tp", self.up_hops)

    def down(self, value):
        return lax.ppermute(value, "tp", self.down_hops)

    def index_at(self, distance):
        place = lax.rem(self.spot + distance + 2 * self.n, self.n)
        return jnp.where(place < self.m, 2 * place, 2 * (self.n - 1 - place) + 1)

    def pair(self, distance):
        first, second = self.index_at(distance), self.index_at(distance - self.m)
        mine = first // self.m == self.core
        return mine, jnp.where(mine, first, second) - self.core * self.m


def swap_cores(value):
    return lax.ppermute(value, "dp", [(0, 1), (1, 0)])


def after(values, done):
    return lax.optimization_barrier((values, done))[0]


def dot(left, right, left_dim, right_dim):
    return lax.dot_general(left, right, (((left_dim,), (right_dim,)), ((), ())), preferred_element_type=F32)


class Gather:
    def __init__(self, ring, own, far_up):
        self.ring, self.far_up = ring, far_up
        self.blocks = {0: own}
        shape = (own.shape[0], own.shape[1] * ring.m)
        self.own, self.got = jnp.zeros(shape, own.dtype), jnp.zeros(shape, own.dtype)
        self.step = 0

    def advance(self, done):
        ring, s = self.ring, self.step
        behind, ahead = after((self.blocks[-s], self.blocks[s]), done)
        s = self.step = s + 1
        if s < ring.m:
            self.blocks[-s], self.blocks[s] = ring.up(behind), ring.down(ahead)
        else:
            self.blocks[-s] = self.blocks[s] = ring.up(behind) if self.far_up else ring.down(ahead)
        return behind

    def swap(self, step, mark):
        ring = self.ring
        width = self.blocks[0].shape[1]
        made = []
        for d in range(1, ring.m + 1):
            if max(d, ring.m - d) == step:
                mine, block = ring.pair(d)
                first, second = after((self.blocks[d], self.blocks[d - ring.m]), mark)
                keep, send = jnp.where(mine, first, second), jnp.where(mine, second, first)
                self.own = lax.dynamic_update_slice(self.own, keep, (0, block * width))
                self.got = lax.dynamic_update_slice(self.got, swap_cores(send), (0, block * width))
                made.append(send)
        return made


class Terms:
    def __init__(self, ring, term_of):
        self.ring, self.term_of, self.made = ring, term_of, {}

    def work_out(self, pairs, mark):
        results = []
        for d in pairs:
            if d in self.made or d <= 0:
                continue
            mine, block = self.ring.pair(d)
            own, other = self.term_of(block, mark)
            got = swap_cores(other)
            self.made[d] = (mine, own, got)
            self.made[d - self.ring.m] = (mine, got, own)
            results.append(other)
        return results

    def __getitem__(self, distance):
        return jnp.where(*self.made[distance])


class Sum:
    def __init__(self, ring, terms, far_up):
        self.ring, self.terms, self.far_up = ring, terms, far_up
        self.distance = ring.m
        self.ahead = self.behind = None

    def advance(self, done):
        ring, distance = self.ring, self.distance
        self.distance -= 1
        if distance == ring.m:
            far = after(self.terms[distance], done)
            if self.far_up:
                self.ahead = ring.up(far)
            else:
                self.behind = ring.down(far)
            return far
        ahead, behind = self.terms[distance], self.terms[-distance]
        if self.ahead is not None:
            ahead = ahead + self.ahead
        if self.behind is not None:
            behind = behind + self.behind
        ahead, behind = after((ahead, behind), done)
        self.ahead, self.behind = ring.up(ahead), ring.down(behind)
        return behind

    def total(self):
        return self.terms[0].astype(F32) + self.ahead.astype(F32) + self.behind.astype(F32)


def body(n, tokens, gate_weight, up_weight, down_weight, out_grad):
    ring = Ring(n)
    m, rows, width = n // 2, tokens.shape[0], tokens.shape[1]

    def rows_of(weight, block):
        return lax.dynamic_slice_in_dim(weight, block * width, width, 0)

    def columns_of(weight, block):
        return lax.dynamic_slice_in_dim(weight, block * width, width, 1)

    t, g = Gather(ring, tokens, True), Gather(ring, out_grad, False)
    done = []
    for step in range(1, m + 1):
        mark = t.advance(done)
        done = t.swap(step - 1, mark)
        mark = g.advance(done)
        done = g.swap(step - 1, mark)
    t.swap(m, done)
    gate_own, up_own = dot(t.own, gate_weight, 1, 0), dot(t.own, up_weight, 1, 0)
    t_got = after(t.got, (gate_own, up_own))
    gate_other, up_other = dot(t_got, gate_weight, 1, 0).astype(BF16), dot(t_got, up_weight, 1, 0).astype(BF16)
    gate_got, up_got = swap_cores(gate_other), swap_cores(up_other)
    g.swap(m, gate_own)
    g_own, g_got = after((g.own, g.got), (gate_other, up_other))
    grad_other = dot(g_got, down_weight, 1, 1).astype(BF16)
    grad_got = swap_cores(grad_other)
    grad_own = dot(g_own, down_weight, 1, 1)

    gate_value, up_value = gate_own + gate_got.astype(F32), up_own + up_got.astype(F32)
    sigmoid_gate = jax.nn.sigmoid(gate_value)
    activated = gate_value * sigmoid_gate
    slope = up_value * sigmoid_gate * (1.0 + gate_value * (1.0 - sigmoid_gate))
    hidden = (activated * up_value).astype(BF16)
    activated, slope, hidden = lax.optimization_barrier((activated, slope, hidden))
    hidden_got = swap_cores(hidden)
    hidden_grad = after(grad_own, hidden) + grad_got.astype(F32)
    gate_grad, up_grad = (hidden_grad * slope).astype(BF16), (hidden_grad * activated).astype(BF16)
    gate_grad, up_grad = lax.optimization_barrier((gate_grad, up_grad))
    gate_grad_got, up_grad_got = swap_cores(gate_grad), swap_cores(up_grad)
    hidden_both = jnp.concatenate([hidden, hidden_got], 0)
    gate_both = jnp.concatenate([gate_grad, gate_grad_got], 0)
    up_both = jnp.concatenate([up_grad, up_grad_got], 0)

    def output_term(block, mark):
        h = after(hidden_both, mark)
        both = dot(h, columns_of(down_weight, block), 1, 0).astype(BF16)
        return both[:rows], both[rows:]

    def input_term(block, mark):
        a, b = after((gate_both, up_both), mark)
        both = (dot(a, rows_of(gate_weight, block), 1, 1) + dot(b, rows_of(up_weight, block), 1, 1)).astype(BF16)
        return both[:rows], both[rows:]

    tokens_half = jnp.concatenate([t.own, t.got], 0)
    grad_half = jnp.concatenate([g.own, g.got], 0)
    wgrads = []
    pieces = [
        lambda mark: dot(after(hidden_both, mark), grad_half, 0, 0).astype(BF16),
        lambda mark: dot(tokens_half, after(gate_both, mark), 0, 0).astype(BF16),
        lambda mark: dot(tokens_half, after(up_both, mark), 0, 0).astype(BF16),
    ]

    def wgrad_work(mark):
        wgrads.append(pieces[len(wgrads)](mark))
        return [wgrads[-1]]

    o, i = Terms(ring, output_term), Terms(ring, input_term)
    o.work_out([m], [])
    i.work_out([m], o.made[m][1])
    o_sum, i_sum = Sum(ring, o, True), Sum(ring, i, False)
    mark = o_sum.advance([])
    done = o.work_out([m - 1, 1], (mark, i.made[m][1]))
    mark = i_sum.advance(done)
    done = i.work_out([m - 1], mark)
    for distance in range(m - 1, 0, -1):
        mark = o_sum.advance(done)
        done = i.work_out([m - distance], mark)
        if distance <= 2:
            done += wgrad_work(mark)
        mark = i_sum.advance(done)
        pairs = [distance - 1, m - distance + 1]
        done = o.work_out(pairs, mark) + i.work_out(pairs[:1], mark)
        if distance == 1:
            wgrad_work(mark)
    output, input_grad = o_sum.total(), i_sum.total()
    return output.astype(BF16), input_grad.astype(BF16), wgrads[1], wgrads[2], wgrads[0]


def solution(mesh):
    n = mesh.shape["tp"]
    rows = P(("rep", "dp"), "tp")
    in_specs = (rows, P("dp", "tp"), P("dp", "tp"), P("tp", "dp"), rows)
    out_specs = (rows, rows, rows, rows, P("tp", ("rep", "dp")))

    def call(*args):
        return body(n, *args)

    return jax.shard_map(call, mesh=mesh, in_specs=in_specs, out_specs=out_specs, check_vma=False)
```

```python
import jax
import jax.numpy as jnp
from jax import lax
from jax.sharding import PartitionSpec as P

BF16 = jnp.bfloat16
F32 = jnp.float32


def hops(n):
    order = list(range(0, n, 2)) + list(range(n - 1, 0, -2))
    up = [(order[i], order[(i + 1) % n]) for i in range(n)]
    return up, [(b, a) for a, b in up]


class Ring:
    def __init__(self, n):
        self.n, self.m = n, n // 2
        self.up_hops, self.down_hops = hops(n)
        index = lax.axis_index("tp")
        self.core = lax.axis_index("dp")
        self.spot = jnp.where(lax.rem(index, 2) == 0, index // 2, n - 1 - index // 2)

    def up(self, value):
        return lax.ppermute(value, "tp", self.up_hops)

    def down(self, value):
        return lax.ppermute(value, "tp", self.down_hops)

    def index_at(self, distance):
        place = lax.rem(self.spot + distance + 2 * self.n, self.n)
        return jnp.where(place < self.m, 2 * place, 2 * (self.n - 1 - place) + 1)

    def pair(self, distance):
        first, second = self.index_at(distance), self.index_at(distance - self.m)
        mine = first // self.m == self.core
        return mine, jnp.where(mine, first, second) - self.core * self.m


def swap_cores(value):
    return lax.ppermute(value, "dp", [(0, 1), (1, 0)])


def after(values, done):
    return lax.optimization_barrier((values, done))[0]


def dot(left, right, left_dim, right_dim):
    return lax.dot_general(left, right, (((left_dim,), (right_dim,)), ((), ())), preferred_element_type=F32)


class Gather:
    def __init__(self, ring, own, far_up):
        self.ring, self.far_up = ring, far_up
        self.blocks = {0: own}
        shape = (own.shape[0], own.shape[1] * ring.m)
        self.own, self.got = jnp.zeros(shape, own.dtype), jnp.zeros(shape, own.dtype)
        self.step = 0

    def advance(self, done):
        ring, s = self.ring, self.step
        behind, ahead = after((self.blocks[-s], self.blocks[s]), done)
        s = self.step = s + 1
        if s < ring.m:
            self.blocks[-s], self.blocks[s] = ring.up(behind), ring.down(ahead)
        else:
            self.blocks[-s] = self.blocks[s] = ring.up(behind) if self.far_up else ring.down(ahead)
        return behind

    def swap(self, step, mark):
        ring = self.ring
        width = self.blocks[0].shape[1]
        made = []
        for d in range(1, ring.m + 1):
            if max(d, ring.m - d) == step:
                mine, block = ring.pair(d)
                first, second = after((self.blocks[d], self.blocks[d - ring.m]), mark)
                keep, send = jnp.where(mine, first, second), jnp.where(mine, second, first)
                self.own = lax.dynamic_update_slice(self.own, keep, (0, block * width))
                self.got = lax.dynamic_update_slice(self.got, swap_cores(send), (0, block * width))
                made.append(send)
        return made


class Terms:
    def __init__(self, ring, term_of):
        self.ring, self.term_of, self.made = ring, term_of, {}

    def work_out(self, pairs, mark):
        results = []
        for d in pairs:
            if d in self.made or d <= 0:
                continue
            mine, block = self.ring.pair(d)
            own, other = self.term_of(block, mark)
            got = swap_cores(other)
            self.made[d] = (mine, own, got)
            self.made[d - self.ring.m] = (mine, got, own)
            results.append(other)
        return results

    def __getitem__(self, distance):
        return jnp.where(*self.made[distance])


class Sum:
    def __init__(self, ring, terms, far_up):
        self.ring, self.terms, self.far_up = ring, terms, far_up
        self.distance = ring.m
        self.ahead = self.behind = None

    def advance(self, done):
        ring, distance = self.ring, self.distance
        self.distance -= 1
        if distance == ring.m:
            far = after(self.terms[distance], done)
            if self.far_up:
                self.ahead = ring.up(far)
            else:
                self.behind = ring.down(far)
            return far
        ahead, behind = self.terms[distance], self.terms[-distance]
        if self.ahead is not None:
            ahead = ahead + self.ahead
        if self.behind is not None:
            behind = behind + self.behind
        ahead, behind = after((ahead, behind), done)
        self.ahead, self.behind = ring.up(ahead), ring.down(behind)
        return behind

    def total(self):
        return self.terms[0].astype(F32) + self.ahead.astype(F32) + self.behind.astype(F32)


def body(n, tokens, gate_weight, up_weight, down_weight, out_grad):
    ring = Ring(n)
    m, rows, width = n // 2, tokens.shape[0], tokens.shape[1]

    def rows_of(weight, block):
        return lax.dynamic_slice_in_dim(weight, block * width, width, 0)

    def columns_of(weight, block):
        return lax.dynamic_slice_in_dim(weight, block * width, width, 1)

    t, g = Gather(ring, tokens, True), Gather(ring, out_grad, False)
    done = []
    for step in range(1, m + 1):
        mark = t.advance(done)
        done = t.swap(step - 1, mark)
        mark = g.advance(done)
        done = g.swap(step - 1, mark)
    t.swap(m, done)
    gate_own, up_own = dot(t.own, gate_weight, 1, 0), dot(t.own, up_weight, 1, 0)
    gate_other, up_other = dot(t.got, gate_weight, 1, 0).astype(BF16), dot(t.got, up_weight, 1, 0).astype(BF16)
    gate_got, up_got = swap_cores(gate_other), swap_cores(up_other)
    g.swap(m, gate_own)
    g_own, g_got = after((g.own, g.got), (gate_other, up_other))
    grad_other = dot(g_got, down_weight, 1, 1).astype(BF16)
    grad_own = dot(g_own, down_weight, 1, 1)
    grad_got = swap_cores(grad_other)

    gate_value, up_value = gate_own + gate_got.astype(F32), up_own + up_got.astype(F32)
    sigmoid_gate = jax.nn.sigmoid(gate_value)
    activated = gate_value * sigmoid_gate
    slope = up_value * sigmoid_gate * (1.0 + gate_value * (1.0 - sigmoid_gate))
    hidden = (activated * up_value).astype(BF16)
    activated, slope = activated.astype(BF16), slope.astype(BF16)
    activated, slope, hidden = lax.optimization_barrier((activated, slope, hidden))
    hidden_got = swap_cores(hidden)
    hidden_grad = after(grad_own, hidden) + grad_got.astype(F32)
    gate_grad = (hidden_grad * slope.astype(F32)).astype(BF16)
    up_grad = (hidden_grad * activated.astype(F32)).astype(BF16)
    gate_grad, up_grad = lax.optimization_barrier((gate_grad, up_grad))
    gate_grad_got, up_grad_got = swap_cores(gate_grad), swap_cores(up_grad)
    hidden_both = jnp.concatenate([hidden, hidden_got], 0)
    gate_both = jnp.concatenate([gate_grad, gate_grad_got], 0)
    up_both = jnp.concatenate([up_grad, up_grad_got], 0)

    def output_term(block, mark):
        h = after(hidden_both, mark)
        both = dot(h, columns_of(down_weight, block), 1, 0).astype(BF16)
        return both[:rows], both[rows:]

    def input_term(block, mark):
        a, b = after((gate_both, up_both), mark)
        both = (dot(a, rows_of(gate_weight, block), 1, 1) + dot(b, rows_of(up_weight, block), 1, 1)).astype(BF16)
        return both[:rows], both[rows:]

    tokens_half = jnp.concatenate([t.own, t.got], 0)
    grad_half = jnp.concatenate([g.own, g.got], 0)
    wgrads = []
    pieces = [
        lambda mark: dot(after(hidden_both, mark), grad_half, 0, 0).astype(BF16),
        lambda mark: dot(tokens_half, after(gate_both, mark), 0, 0).astype(BF16),
        lambda mark: dot(tokens_half, after(up_both, mark), 0, 0).astype(BF16),
    ]

    def wgrad_work(mark):
        wgrads.append(pieces[len(wgrads)](mark))
        return [wgrads[-1]]

    o, i = Terms(ring, output_term), Terms(ring, input_term)
    o_sum, i_sum = Sum(ring, o, True), Sum(ring, i, False)
    o.work_out([m], [])
    i.work_out([m], o.made[m][1])
    mark = o_sum.advance([])
    done = o.work_out([m - 1, 1], (mark, i.made[m][1]))
    mark = i_sum.advance(done)
    done = i.work_out([m - 1], mark)
    for distance in range(m - 1, 0, -1):
        mark = o_sum.advance(done)
        done = i.work_out([m - distance, distance], mark)
        if distance <= 2:
            done += wgrad_work(mark)
        mark = i_sum.advance(done)
        pairs = [distance - 1, m - distance + 1]
        done = o.work_out(pairs, mark) + i.work_out(pairs[:1], mark)
    wgrad_work((mark, o_sum.ahead))
    output, input_grad = o_sum.total(), i_sum.total()
    return output.astype(BF16), input_grad.astype(BF16), wgrads[1], wgrads[2], wgrads[0]


def solution(mesh):
    n = mesh.shape["tp"]
    rows = P(("rep", "dp"), "tp")
    in_specs = (rows, P("dp", "tp"), P("dp", "tp"), P("tp", "dp"), rows)
    out_specs = (rows, rows, rows, rows, P("tp", ("rep", "dp")))

    def call(*args):
        return body(n, *args)

    return jax.shard_map(call, mesh=mesh, in_specs=in_specs, out_specs=out_specs, check_vma=False)
```

```python
import jax
import jax.numpy as jnp
from jax import lax
from jax.sharding import PartitionSpec as P

BF16 = jnp.bfloat16
F32 = jnp.float32


def hops(n):
    order = list(range(0, n, 2)) + list(range(n - 1, 0, -2))
    up = [(order[i], order[(i + 1) % n]) for i in range(n)]
    return up, [(b, a) for a, b in up]


class Ring:
    def __init__(self, n):
        self.n, self.m = n, n // 2
        self.up_hops, self.down_hops = hops(n)
        index = lax.axis_index("tp")
        self.core = lax.axis_index("dp")
        self.spot = jnp.where(lax.rem(index, 2) == 0, index // 2, n - 1 - index // 2)

    def up(self, value):
        return lax.ppermute(value, "tp", self.up_hops)

    def down(self, value):
        return lax.ppermute(value, "tp", self.down_hops)

    def index_at(self, distance):
        place = lax.rem(self.spot + distance + 2 * self.n, self.n)
        return jnp.where(place < self.m, 2 * place, 2 * (self.n - 1 - place) + 1)

    def pair(self, distance):
        first, second = self.index_at(distance), self.index_at(distance - self.m)
        mine = first // self.m == self.core
        return mine, jnp.where(mine, first, second) - self.core * self.m


def swap_cores(value):
    return lax.ppermute(value, "dp", [(0, 1), (1, 0)])


def after(values, done):
    return lax.optimization_barrier((values, done))[0]


def dot(left, right, left_dim, right_dim):
    return lax.dot_general(left, right, (((left_dim,), (right_dim,)), ((), ())), preferred_element_type=F32)


class Gather:
    def __init__(self, ring, own, far_up):
        self.ring, self.far_up = ring, far_up
        self.blocks = {0: own}
        shape = (own.shape[0], own.shape[1] * ring.m)
        self.own, self.got = jnp.zeros(shape, own.dtype), jnp.zeros(shape, own.dtype)
        self.step = 0

    def advance(self, done):
        ring, s = self.ring, self.step
        behind, ahead = after((self.blocks[-s], self.blocks[s]), done)
        s = self.step = s + 1
        if s < ring.m:
            self.blocks[-s], self.blocks[s] = ring.up(behind), ring.down(ahead)
        else:
            self.blocks[-s] = self.blocks[s] = ring.up(behind) if self.far_up else ring.down(ahead)
        return behind

    def swap(self, step, mark):
        ring = self.ring
        width = self.blocks[0].shape[1]
        made = []
        for d in range(1, ring.m + 1):
            if max(d, ring.m - d) == step:
                mine, block = ring.pair(d)
                first, second = after((self.blocks[d], self.blocks[d - ring.m]), mark)
                keep, send = jnp.where(mine, first, second), jnp.where(mine, second, first)
                self.own = lax.dynamic_update_slice(self.own, keep, (0, block * width))
                self.got = lax.dynamic_update_slice(self.got, swap_cores(send), (0, block * width))
                made.append(send)
        return made


class Terms:
    def __init__(self, ring, term_of):
        self.ring, self.term_of, self.made = ring, term_of, {}

    def work_out(self, pairs, mark):
        results = []
        for d in pairs:
            if d in self.made or d <= 0:
                continue
            mine, block = self.ring.pair(d)
            own, other = self.term_of(block, mark)
            got = swap_cores(other)
            self.made[d] = (mine, own, got)
            self.made[d - self.ring.m] = (mine, got, own)
            results.append(other)
        return results

    def __getitem__(self, distance):
        return jnp.where(*self.made[distance])


class Sum:
    def __init__(self, ring, terms, far_up):
        self.ring, self.terms, self.far_up = ring, terms, far_up
        self.distance = ring.m
        self.ahead = self.behind = None

    def advance(self, done):
        ring, distance = self.ring, self.distance
        self.distance -= 1
        if distance == ring.m:
            far = after(self.terms[distance], done)
            if self.far_up:
                self.ahead = ring.up(far)
            else:
                self.behind = ring.down(far)
            return far
        ahead, behind = self.terms[distance], self.terms[-distance]
        if self.ahead is not None:
            ahead = ahead + self.ahead
        if self.behind is not None:
            behind = behind + self.behind
        ahead, behind = after((ahead, behind), done)
        self.ahead, self.behind = ring.up(ahead), ring.down(behind)
        return behind

    def total(self):
        return self.terms[0].astype(F32) + self.ahead.astype(F32) + self.behind.astype(F32)


def body(n, tokens, gate_weight, up_weight, down_weight, out_grad):
    ring = Ring(n)
    m, rows, width = n // 2, tokens.shape[0], tokens.shape[1]

    def rows_of(weight, block):
        return lax.dynamic_slice_in_dim(weight, block * width, width, 0)

    def columns_of(weight, block):
        return lax.dynamic_slice_in_dim(weight, block * width, width, 1)

    t, g = Gather(ring, tokens, True), Gather(ring, out_grad, False)
    done = []
    for step in range(1, m + 1):
        mark = t.advance(done)
        done = t.swap(step - 1, mark)
        mark = g.advance(done)
        done = g.swap(step - 1, mark)
    t.swap(m, done)
    gate_own, up_own = dot(t.own, gate_weight, 1, 0), dot(t.own, up_weight, 1, 0)
    gate_other, up_other = dot(t.got, gate_weight, 1, 0).astype(BF16), dot(t.got, up_weight, 1, 0).astype(BF16)
    gate_got, up_got = swap_cores(gate_other), swap_cores(up_other)
    g.swap(m, gate_own)
    g_own, g_got = after((g.own, g.got), (gate_other, up_other))
    grad_own = dot(g_own, down_weight, 1, 1)
    grad_other = dot(g_got, down_weight, 1, 1).astype(BF16)
    grad_got = swap_cores(grad_other)

    gate_value, up_value = gate_own + gate_got.astype(F32), up_own + up_got.astype(F32)
    sigmoid_gate = jax.nn.sigmoid(gate_value)
    activated = gate_value * sigmoid_gate
    slope = up_value * sigmoid_gate * (1.0 + gate_value * (1.0 - sigmoid_gate))
    hidden = (activated * up_value).astype(BF16)
    activated, slope = activated.astype(BF16), slope.astype(BF16)
    activated, slope, hidden = lax.optimization_barrier((activated, slope, hidden))
    hidden_got = swap_cores(hidden)
    hidden_grad = after(grad_own, hidden) + grad_got.astype(F32)
    gate_grad = (hidden_grad * slope.astype(F32)).astype(BF16)
    up_grad = (hidden_grad * activated.astype(F32)).astype(BF16)
    gate_grad, up_grad = lax.optimization_barrier((gate_grad, up_grad))
    gate_grad_got, up_grad_got = swap_cores(gate_grad), swap_cores(up_grad)
    hidden_both = jnp.concatenate([hidden, hidden_got], 0)
    gate_both = jnp.concatenate([gate_grad, gate_grad_got], 0)
    up_both = jnp.concatenate([up_grad, up_grad_got], 0)

    def output_term(block, mark):
        h = after(hidden_both, mark)
        both = dot(h, columns_of(down_weight, block), 1, 0).astype(BF16)
        return both[:rows], both[rows:]

    def input_term(block, mark):
        a, b = after((gate_both, up_both), mark)
        both = (dot(a, rows_of(gate_weight, block), 1, 1) + dot(b, rows_of(up_weight, block), 1, 1)).astype(BF16)
        return both[:rows], both[rows:]

    tokens_half = jnp.concatenate([t.own, t.got], 0)
    grad_half = jnp.concatenate([g.own, g.got], 0)
    wgrads = []
    pieces = [
        lambda mark: dot(after(hidden_both, mark), grad_half, 0, 0).astype(BF16),
        lambda mark: dot(tokens_half, after(gate_both, mark), 0, 0).astype(BF16),
        lambda mark: dot(tokens_half, after(up_both, mark), 0, 0).astype(BF16),
    ]

    def wgrad_work(mark):
        wgrads.append(pieces[len(wgrads)](mark))
        return [wgrads[-1]]

    o, i = Terms(ring, output_term), Terms(ring, input_term)
    o_sum, i_sum = Sum(ring, o, True), Sum(ring, i, False)
    o.work_out([m], [])
    i.work_out([m], o.made[m][1])
    mark = o_sum.advance([])
    done = o.work_out([m - 1, 1], (mark, i.made[m][1]))
    mark = i_sum.advance(done)
    done = i.work_out([m - 1], mark)
    for distance in range(m - 1, 0, -1):
        mark = o_sum.advance(done)
        done = i.work_out([m - distance, distance], mark)
        if distance <= 2:
            done += wgrad_work(mark)
        mark = i_sum.advance(done)
        pairs = [distance - 1, m - distance + 1]
        done = o.work_out(pairs, mark)
        done += i.work_out(pairs[:1], (mark, done))
    wgrad_work((mark, o_sum.ahead))
    output, input_grad = o_sum.total(), i_sum.total()
    return output.astype(BF16), input_grad.astype(BF16), wgrads[1], wgrads[2], wgrads[0]


def solution(mesh):
    n = mesh.shape["tp"]
    rows = P(("rep", "dp"), "tp")
    in_specs = (rows, P("dp", "tp"), P("dp", "tp"), P("tp", "dp"), rows)
    out_specs = (rows, rows, rows, rows, P("tp", ("rep", "dp")))

    def call(*args):
        return body(n, *args)

    return jax.shard_map(call, mesh=mesh, in_specs=in_specs, out_specs=out_specs, check_vma=False)
```
